32 devices in a mesh: dp: 4 (over y, x), seq: 8 (over z, core).
Axes of the slice: x: 2, y: 2, z: 4, core: 2. Of those that a mesh axis runs over, the one named last changes fastest.
Arguments:
- tokens: bfloat16 [2, 4096, 1088], P(None, ('dp', 'seq')), may hold values from -6 to 6
- cotangent: bfloat16 [2, 4096, 1088], P(None, ('dp', 'seq')), may hold values from -6 to 6
- w_qkv: bfloat16 [1088, 3264], P('dp', 'seq'), may hold values from -0.1875 to 0.1875
- w_out: bfloat16 [1088, 1088], P('dp', 'seq'), may hold values from -1.5 to 1.5
- w_up: bfloat16 [1088, 4352], P('dp', 'seq'), may hold values from -0.1875 to 0.1875
- w_down: bfloat16 [4352, 1088], P('dp', 'seq'), may hold values from -0.09375 to 0.09375
- gain_one: bfloat16 [1088], P('dp'), may hold values from 0.25 to 1.75
- bias_one: bfloat16 [1088], P('dp'), may hold values from -3 to 3
- gain_two: bfloat16 [1088], P('dp'), may hold values from 0.25 to 1.75
- bias_two: bfloat16 [1088], P('dp'), may hold values from -3 to 3
- lengths: int32 [2, 4, 8], P(None, 'dp'), may hold values from 1 to 896, 1024 in all within a row
- slot_order: int32 [2, 4, 8], P(None, 'dp'), may hold values from 0 to 7, each once within a row
Outputs:
- block_out: bfloat16 [2, 4096, 1088], P(None, ('dp', 'seq'))
- grad_input: bfloat16 [2, 4096, 1088], P(None, ('dp', 'seq'))
- grad_qkv: float32 [1088, 3264], P('dp', 'seq')
- grad_proj: float32 [1088, 1088], P('dp', 'seq')
- grad_up: float32 [1088, 4352], P('dp', 'seq')
- grad_down: float32 [4352, 1088], P('dp', 'seq')
- grad_gain_one: float32 [1088], P('dp')
- grad_bias_one: float32 [1088], P('dp')
- grad_gain_two: float32 [1088], P('dp')
- grad_bias_two: float32 [1088], P('dp')
The draws below stay inside these ranges and needn't reach their ends.
Inputs may be any that keep to these rules, and one draw needn't show every extreme that they name: For each micro-batch and group the 8 lengths sum to 1024; the largest is exactly 896. `slot_order`: each row over the last dimension holds every number below 8 once.
All inputs are finite; a program needn't handle non-finite values.
Results may differ from the reference program's by a relative error of at most 0.02.
Values may be sent and summed in bfloat16 or wider, within the bound.
A program may use at most 192 MiB of HBM per device.

```python
import math
import jax
import jax.numpy as jnp
import numpy as np
from jax import lax

D = 1088
HEADS = 17
HEAD_DIM = 64
FF = 4352
TOK_DEV = 128
MICRO = 2
DOCS = 8
TOK_GROUP = 1024
TOKENS = 4096
MOST = 896
N_DP = 4
N_SEQ = 8


def block_scale(own_key, extent, shards, least, largest):
    level = 1.0
    for axis_at, shards_of in shards:
        steps = jax.random.uniform(jax.random.fold_in(jax.random.fold_in(own_key, 6), axis_at), (shards_of,), jnp.float32, least / len(shards), largest / len(shards))
        level = level * jnp.repeat(jnp.exp(steps), extent[axis_at] // shards_of).reshape((-1,) + (1,) * (len(extent) - 1 - axis_at))
    return level


def split_up(number_of, total, bound, lean):
    weights = [(1 << 20) // math.isqrt(grade ** lean) + 1 for grade in range(2, number_of + 1)]
    surplus, given = total - bound - (number_of - 1), [1] * (number_of - 1)
    while surplus > 0:
        movable = [i for i in range(number_of - 1) if given[i] < bound]
        whole, left = sum([weights[i] for i in movable]), surplus
        for i in movable:
            more = min(bound - given[i], max(1, left * weights[i] // whole), surplus)
            given[i] = given[i] + more
            surplus = surplus - more
    return np.array([bound] + given)


def uneven(key, number_of, total, limit, skew):
    if number_of == 2:
        one = jax.random.randint(key, (), max(1, total - limit), min(limit, total - 1) + 1)
        return jnp.stack([one, total - one])
    tallies = jnp.asarray(split_up(number_of, total, limit, skew), jnp.int32)
    couples = (number_of - 1) // 2
    source_of, taker = tallies[1:1 + 2 * couples:2], tallies[2:2 + 2 * couples:2]
    slack = jnp.minimum(source_of - 1, limit - taker)
    passed = jax.random.randint(jax.random.fold_in(key, 1), (couples,), 0, 1 << 20) % (slack + 1)
    tallies = tallies.at[1:1 + 2 * couples:2].set(source_of - passed).at[2:2 + 2 * couples:2].set(taker + passed)
    return tallies[jax.random.permutation(jax.random.fold_in(key, 2), number_of)]


def normal_values(rng, extent, width, reach, cuts=(), kind=jnp.bfloat16):
    level = block_scale(rng, extent, cuts, -0.22, 0.18) if cuts else 1.0
    values = jax.random.normal(rng, extent, jnp.float32) * width * level
    return jnp.minimum(jnp.maximum(values, -reach), reach).astype(kind)


def setup_inputs(seed: int = 0) -> dict:
    key_list = jax.random.split(jax.random.key(seed), 13)
    return {
        "tokens": normal_values(key_list[0], (MICRO, TOKENS, D), 1.0, 6.0, ((1, 32),)),
        "cotangent": normal_values(key_list[1], (MICRO, TOKENS, D), 1.0, 6.0, ((1, 32),)),
        "w_qkv": normal_values(key_list[2], (D, 3 * D), D ** -0.5, 0.1875, ((0, 4), (1, 8))),
        "w_out": normal_values(key_list[3], (D, D), (max(D // 64, 1)) ** -0.5, 1.5, ((0, 4), (1, 8))),
        "w_up": normal_values(key_list[4], (D, FF), D ** -0.5, 0.1875, ((0, 4), (1, 8))),
        "w_down": normal_values(key_list[5], (FF, D), FF ** -0.5, 0.09375, ((0, 4), (1, 8))),
        "gain_one": jnp.clip(1.0 + 0.15 * jax.random.normal(key_list[6], (D,), jnp.float32), 0.25, 1.75).astype(jnp.bfloat16),
        "bias_one": normal_values(key_list[7], (D,), 0.5, 3.0, ((0, 4),)),
        "gain_two": jnp.clip(1.0 + 0.15 * jax.random.normal(key_list[8], (D,), jnp.float32), 0.25, 1.75).astype(jnp.bfloat16),
        "bias_two": normal_values(key_list[9], (D,), 0.5, 3.0, ((0, 4),)),
        "lengths": jax.vmap(lambda own: uneven(own, DOCS, TOK_GROUP, MOST, 2))(jax.random.split(key_list[10], MICRO * N_DP)).reshape((MICRO, N_DP, DOCS)).astype(jnp.int32),
        "slot_order": jax.vmap(lambda own: jax.random.permutation(own, N_SEQ))(jax.random.split(key_list[11], MICRO * N_DP)).reshape((MICRO, N_DP, N_SEQ)).astype(jnp.int32),
    }


@jax.custom_vjp
def low(v):
    return lax.optimization_barrier(v.astype(jnp.bfloat16)).astype(jnp.float32)

@jax.custom_vjp
def low_back(v):
    return v

def low_keep(v):
    return (low(v), None)

def low_pass(kept, grad):
    return (grad,)

def back_keep(v):
    return (v, None)

def back_low(kept, grad):
    return (low(grad),)
low.defvjp(low_keep, low_pass)
low_back.defvjp(back_keep, back_low)
EPS = 1e-05
NEG = -1e+30
GELU_C = 0.7978845608028654

def matmul_high(left_side, right_side):
    return jnp.dot(left_side, right_side, precision=lax.Precision.HIGHEST, preferred_element_type=jnp.float32)

def layer_norm(residual, gain_row, offset):
    row_mean = lax.optimization_barrier(jnp.mean(residual, -1, keepdims=True))
    centered = residual - row_mean
    variance = lax.optimization_barrier(jnp.mean(centered * centered, -1, keepdims=True))
    return centered * lax.rsqrt(variance + EPS) * gain_row + offset

def gelu_tanh(values):
    return 0.5 * values * (1.0 + jnp.tanh(GELU_C * (values + 0.044715 * values * values * values)))

def attend_block(queries, q_place, q_segment, key_all, value_all, k_place, k_segment):
    scores = jnp.einsum('qhd,khd->hqk', queries, key_all, precision=lax.Precision.HIGHEST) * HEAD_DIM ** (-0.5)
    allowed = (q_segment[:, None] == k_segment[None, :]) & (k_place[None, :] <= q_place[:, None])
    scores = low_back(jnp.where(allowed[None], scores, NEG))
    probabilities = jax.nn.softmax(scores, axis=-1)
    return jnp.einsum('hqk,khd->qhd', low(probabilities), value_all, precision=lax.Precision.HIGHEST)

def group_layer(residual, places, segments, params):
    w_qkv, w_out, w_up, w_down, gain_one, bias_one, gain_two, bias_two = params
    normed = low(layer_norm(residual, gain_one, bias_one))
    qkv_all = low(low_back(matmul_high(normed, w_qkv)))
    queries = qkv_all[:, :D].reshape(TOK_GROUP, HEADS, HEAD_DIM)
    key_all = qkv_all[:, D:2 * D].reshape(TOK_GROUP, HEADS, HEAD_DIM)
    value_all = qkv_all[:, 2 * D:].reshape(TOK_GROUP, HEADS, HEAD_DIM)
    checked = jax.checkpoint(attend_block)

    def per_block(block_item):
        return checked(block_item[0], block_item[1], block_item[2], key_all, value_all, places, segments)
    attended = lax.map(per_block, (queries.reshape(N_SEQ, TOK_DEV, HEADS, HEAD_DIM), places.reshape(N_SEQ, TOK_DEV), segments.reshape(N_SEQ, TOK_DEV)))
    attended = low(low_back(attended.reshape(TOK_GROUP, D)))
    middle = residual + low_back(matmul_high(attended, w_out))
    normed_two = low(layer_norm(middle, gain_two, bias_two))
    hidden = low_back(matmul_high(normed_two, w_up))
    activated = low(gelu_tanh(hidden))
    return middle + matmul_high(activated, w_down)

def reference(tokens, cotangent, w_qkv, w_out, w_up, w_down, gain_one, bias_one, gain_two, bias_two, lengths, slot_order):
    groups = MICRO * N_DP
    resid_all = tokens.astype(jnp.float32).reshape(groups, TOK_GROUP, D)
    order_rows = slot_order.reshape(groups, N_SEQ).astype(jnp.int32)
    places = order_rows[:, :, None] * TOK_DEV + jnp.arange(TOK_DEV, dtype=jnp.int32)[None, None, :]
    places = places.reshape(groups, TOK_GROUP).astype(jnp.int32)
    doc_ends = jnp.cumsum(lengths.reshape(groups, DOCS), axis=-1).astype(jnp.int32)
    segments = lax.optimization_barrier(jnp.sum((places[:, :, None] >= doc_ends[:, None, :]).astype(jnp.int32), axis=-1)).astype(jnp.int32)
    params = (w_qkv.astype(jnp.float32), w_out.astype(jnp.float32), w_up.astype(jnp.float32), w_down.astype(jnp.float32), gain_one.astype(jnp.float32), bias_one.astype(jnp.float32), gain_two.astype(jnp.float32), bias_two.astype(jnp.float32))

    def forward(resid_all, params):

        def per_group(group_item):
            return group_layer(group_item[0], group_item[1], group_item[2], params)
        return lax.map(per_group, (resid_all, places, segments))
    outputs, pullback = jax.vjp(forward, resid_all, params)
    grad_resid, grad_params = pullback(cotangent.astype(jnp.float32).reshape(groups, TOK_GROUP, D))
    return (outputs.astype(jnp.bfloat16).reshape(MICRO, TOKENS, D), grad_resid.astype(jnp.bfloat16).reshape(MICRO, TOKENS, D), grad_params[0], grad_params[1], grad_params[2], grad_params[3], grad_params[4], grad_params[5], grad_params[6], grad_params[7])
```

```python
import jax
import jax.numpy as jnp
from jax import lax
from jax.sharding import PartitionSpec as P

HEADS = 17


EPS = 1e-05
NEG = -1e30
GELU_C = 0.7978845608028654
block_rows = 512


def from_behind(block, axis, distance):
    devices = range(lax.axis_size(axis))
    route = [((i - distance) % len(devices), i) for i in devices]
    return lax.ppermute(block, axis, route)


def gelu_tanh(values):
    return 0.5 * values * (1.0 + jnp.tanh(GELU_C * (values + 0.044715 * values * values * values)))


def normalize(residual):
    row_mean = jnp.mean(residual, -1, keepdims=True)
    centered = residual - row_mean
    inv_std = lax.rsqrt(jnp.mean(centered * centered, -1, keepdims=True) + EPS)
    return (centered * inv_std, inv_std)


def norm_back(grad_normed, scaled, inv_std, gain_row):
    grad_scaled = grad_normed * gain_row
    return inv_std * (
        grad_scaled
        - jnp.mean(grad_scaled, -1, keepdims=True)
        - scaled * jnp.mean(grad_scaled * scaled, -1, keepdims=True)
    )


def running_total(counts):
    index = jnp.arange(counts.shape[0], dtype=jnp.int32)
    return jnp.sum(jnp.where(index[None, :] <= index[:, None], counts[None, :], 0), 1)


def segment_of(places, doc_ends):
    return jnp.sum((places[:, None] >= doc_ends[None, :]).astype(jnp.int32), 1)


def key_places(first_row, key_count, slot_row, doc_ends, tok_dev):
    row_index = first_row + jnp.arange(key_count, dtype=jnp.int32)
    source_slot = row_index // tok_dev
    slot_ids = jnp.arange(slot_row.shape[0], dtype=jnp.int32)
    base_slot = jnp.sum(
        jnp.where(source_slot[:, None] == slot_ids[None, :], slot_row[None, :], 0), 1
    )
    places = base_slot * tok_dev + row_index % tok_dev
    return (places, segment_of(places, doc_ends))


def masked_scores(queries, key_block, q_place, q_segment, k_place, k_segment, score_scale):
    key_heads = key_block.reshape(key_block.shape[0], queries.shape[1], queries.shape[2])
    scores = (
        jnp.einsum("qhd,khd->hqk", queries, key_heads, preferred_element_type=jnp.float32)
        * score_scale
    )
    allowed = (q_segment[:, None] == k_segment[None, :]) & (k_place[None, :] <= q_place[:, None])
    return (jnp.where(allowed[None], scores, -jnp.inf), key_heads)


def fold_keys(state_now, key_block, value_block, first_row, context):
    queries, q_place, q_segment, slot_row, doc_ends, score_scale = context
    running_max, running_sum, accum_out = state_now
    k_place, k_segment = key_places(
        first_row, key_block.shape[0], slot_row, doc_ends, queries.shape[0]
    )
    scores, key_heads = masked_scores(
        queries, key_block, q_place, q_segment, k_place, k_segment, score_scale
    )
    value_heads = value_block.reshape(key_heads.shape)
    new_max = jnp.maximum(running_max, jnp.max(scores, -1))
    weights = jnp.exp(scores - new_max[..., None])
    factor = jnp.exp(running_max - new_max)
    running_sum = running_sum * factor + jnp.sum(weights, -1)
    accum_out = accum_out * factor.T[:, :, None] + jnp.einsum(
        "hqk,khd->qhd",
        weights.astype(jnp.bfloat16),
        value_heads,
        preferred_element_type=jnp.float32,
    )
    return (new_max, running_sum, accum_out)


def back_block(
    queries,
    grad_heads,
    key_block,
    value_block,
    q_place,
    q_segment,
    k_place,
    k_segment,
    log_sum,
    row_dot,
    score_scale,
):
    scores, key_heads = masked_scores(
        queries, key_block, q_place, q_segment, k_place, k_segment, score_scale
    )
    value_heads = value_block.reshape(key_heads.shape)
    probabilities = jnp.exp(scores - log_sum[..., None])
    grad_probs = jnp.einsum(
        "qhd,khd->hqk", grad_heads, value_heads, preferred_element_type=jnp.float32
    )
    grad_scores = (probabilities * (grad_probs - row_dot[..., None])).astype(jnp.bfloat16)
    grad_query = score_scale * jnp.einsum(
        "hqk,khd->qhd", grad_scores, key_heads, preferred_element_type=jnp.float32
    )
    grad_keys = score_scale * jnp.einsum(
        "hqk,qhd->khd", grad_scores, queries, preferred_element_type=jnp.float32
    )
    grad_values = jnp.einsum(
        "hqk,qhd->khd",
        probabilities.astype(jnp.bfloat16),
        grad_heads,
        preferred_element_type=jnp.float32,
    )
    return (grad_query, grad_keys.reshape(key_block.shape), grad_values.reshape(key_block.shape))


def shards(
    tokens,
    cotangent,
    w_qkv,
    w_out,
    w_up,
    w_down,
    gain_one,
    bias_one,
    gain_two,
    bias_two,
    lengths,
    slot_order,
):
    micro_count, tok_dev, width = tokens.shape
    head_dim = width // HEADS
    score_scale = head_dim ** (-0.5)
    n_seq = lax.axis_size("seq")
    my_slot = lax.axis_index("seq")
    slot_ids = jnp.arange(n_seq, dtype=jnp.int32)
    ffn_width = w_up.shape[1] * n_seq
    sum_qkv = jnp.zeros((width, 3 * width), jnp.float32)
    sum_out = jnp.zeros((width, width), jnp.float32)
    sum_up = jnp.zeros((width, ffn_width), jnp.float32)
    sum_down = jnp.zeros((ffn_width, width), jnp.float32)
    sum_gain_one = jnp.zeros((width,), jnp.float32)
    sum_bias_one = jnp.zeros((width,), jnp.float32)
    sum_gain_two = jnp.zeros((width,), jnp.float32)
    sum_bias_two = jnp.zeros((width,), jnp.float32)
    out_rows = []
    input_grads = []
    for micro_index in range(micro_count):
        col_parts = (
            lax.all_gather(w_qkv, "seq", axis=1, tiled=True),
            lax.all_gather(w_out, "seq", axis=1, tiled=True),
            lax.all_gather(w_up, "seq", axis=1, tiled=True),
            lax.all_gather(w_down, "seq", axis=1, tiled=True),
        )
        full_qkv, full_out, full_up, full_down, g_one, b_one, g_two, b_two = (
            lax.all_gather(col_parts[0], "dp", axis=0, tiled=True),
            lax.all_gather(col_parts[1], "dp", axis=0, tiled=True),
            lax.all_gather(col_parts[2], "dp", axis=0, tiled=True),
            lax.all_gather(col_parts[3], "dp", axis=0, tiled=True),
            lax.all_gather(gain_one, "dp", axis=0, tiled=True),
            lax.all_gather(bias_one, "dp", axis=0, tiled=True),
            lax.all_gather(gain_two, "dp", axis=0, tiled=True),
            lax.all_gather(bias_two, "dp", axis=0, tiled=True),
        )
        slot_row = slot_order[micro_index, 0]
        doc_ends = running_total(lengths[micro_index, 0])
        base_slot = jnp.sum(jnp.where(slot_ids == my_slot, slot_row, 0))
        q_place = base_slot * tok_dev + jnp.arange(tok_dev, dtype=jnp.int32)
        q_segment = segment_of(q_place, doc_ends)
        residual = tokens[micro_index].astype(jnp.float32)
        scaled_one, inv_one = normalize(residual)
        normed_one = (scaled_one * g_one.astype(jnp.float32) + b_one.astype(jnp.float32)).astype(
            jnp.bfloat16
        )
        qkv_all = jnp.dot(normed_one, full_qkv, preferred_element_type=jnp.float32).astype(
            jnp.bfloat16
        )
        queries = qkv_all[:, :width].reshape(tok_dev, HEADS, head_dim)
        key_local = qkv_all[:, width : 2 * width]
        value_local = qkv_all[:, 2 * width :]
        context = (queries, q_place, q_segment, slot_row, doc_ends, score_scale)

        def attend(state_now, key_piece, first_row, context=context):
            key_part, value_part = key_piece
            key_count = key_part.shape[0]
            blocks = key_count // block_rows

            def scan_step(inner_state, block_item):
                return (
                    fold_keys(
                        inner_state,
                        block_item[0],
                        block_item[1],
                        block_item[2] * block_rows,
                        context,
                    ),
                    None,
                )

            final_state, _ = lax.scan(
                scan_step,
                state_now,
                (
                    key_part.reshape(blocks, block_rows, width),
                    value_part.reshape(blocks, block_rows, width),
                    jnp.arange(blocks, dtype=jnp.int32),
                ),
            )
            return final_state

        start_state = (
            jnp.full((HEADS, tok_dev), NEG, jnp.float32),
            jnp.zeros((HEADS, tok_dev), jnp.float32),
            jnp.zeros((tok_dev, HEADS, head_dim), jnp.float32),
        )
        running_max, running_sum, accum_out = attend(
            start_state,
            (
                lax.all_gather(key_local, "seq", axis=0, tiled=True),
                lax.all_gather(value_local, "seq", axis=0, tiled=True),
            ),
            jnp.int32(0),
        )
        attended = accum_out / running_sum.T[:, :, None]
        log_sum = running_max + jnp.log(running_sum)
        attn_flat = attended.reshape(tok_dev, width).astype(jnp.bfloat16)
        middle = residual + jnp.dot(attn_flat, full_out, preferred_element_type=jnp.float32)
        scaled_two, inv_two = normalize(middle)
        normed_two = (scaled_two * g_two.astype(jnp.float32) + b_two.astype(jnp.float32)).astype(
            jnp.bfloat16
        )
        hidden = jnp.dot(normed_two, full_up, preferred_element_type=jnp.float32)
        activated_full, gelu_back = jax.vjp(gelu_tanh, hidden)
        activated = activated_full.astype(jnp.bfloat16)
        block_out = middle + jnp.dot(activated, full_down, preferred_element_type=jnp.float32)
        out_rows.append(block_out.astype(jnp.bfloat16))
        back_parts = (
            lax.all_gather(w_qkv, "seq", axis=1, tiled=True),
            lax.all_gather(w_out, "seq", axis=1, tiled=True),
            lax.all_gather(w_up, "seq", axis=1, tiled=True),
            lax.all_gather(w_down, "seq", axis=1, tiled=True),
        )
        back_qkv, back_out, back_up, back_down, back_gain_one, back_gain_two = (
            lax.all_gather(back_parts[0], "dp", axis=0, tiled=True),
            lax.all_gather(back_parts[1], "dp", axis=0, tiled=True),
            lax.all_gather(back_parts[2], "dp", axis=0, tiled=True),
            lax.all_gather(back_parts[3], "dp", axis=0, tiled=True),
            lax.all_gather(gain_one, "dp", axis=0, tiled=True),
            lax.all_gather(gain_two, "dp", axis=0, tiled=True),
        )
        grad_rows = cotangent[micro_index]
        sum_down = sum_down + jnp.einsum(
            "tf,td->fd", activated, grad_rows, preferred_element_type=jnp.float32
        )
        grad_act = jnp.einsum("td,fd->tf", grad_rows, back_down, preferred_element_type=jnp.float32)
        grad_hidden = gelu_back(grad_act)[0].astype(jnp.bfloat16)
        sum_up = sum_up + jnp.einsum(
            "td,tf->df", normed_two, grad_hidden, preferred_element_type=jnp.float32
        )
        grad_normed_two = jnp.einsum(
            "tf,df->td", grad_hidden, back_up, preferred_element_type=jnp.float32
        )
        sum_gain_two = sum_gain_two + jnp.sum(grad_normed_two * scaled_two, 0)
        sum_bias_two = sum_bias_two + jnp.sum(grad_normed_two, 0)
        grad_middle = grad_rows.astype(jnp.float32) + norm_back(
            grad_normed_two, scaled_two, inv_two, back_gain_two.astype(jnp.float32)
        )
        grad_branch = grad_middle.astype(jnp.bfloat16)
        sum_out = sum_out + jnp.einsum(
            "td,te->de", attn_flat, grad_branch, preferred_element_type=jnp.float32
        )
        grad_attn = jnp.einsum(
            "te,de->td", grad_branch, back_out, preferred_element_type=jnp.float32
        ).astype(jnp.bfloat16)
        grad_heads = grad_attn.reshape(tok_dev, HEADS, head_dim)
        row_dot = jnp.einsum("qhd,qhd->hq", grad_heads.astype(jnp.float32), attended)
        stacked = jnp.stack(
            [
                key_local.astype(jnp.float32),
                value_local.astype(jnp.float32),
                jnp.zeros((tok_dev, width), jnp.float32),
                jnp.zeros((tok_dev, width), jnp.float32),
            ]
        )

        def return_step(
            step_index,
            loop_state,
            queries=queries,
            grad_heads=grad_heads,
            q_place=q_place,
            q_segment=q_segment,
            slot_row=slot_row,
            doc_ends=doc_ends,
            log_sum=log_sum,
            row_dot=row_dot,
        ):
            carried, grad_query = loop_state
            source = (my_slot - step_index) % n_seq
            k_place, k_segment = key_places(source * tok_dev, tok_dev, slot_row, doc_ends, tok_dev)
            part_query, part_keys, part_values = back_block(
                queries,
                grad_heads,
                carried[0].astype(jnp.bfloat16),
                carried[1].astype(jnp.bfloat16),
                q_place,
                q_segment,
                k_place,
                k_segment,
                log_sum,
                row_dot,
                score_scale,
            )
            carried = jnp.stack(
                [carried[0], carried[1], carried[2] + part_keys, carried[3] + part_values]
            )
            carried = from_behind(carried.astype(jnp.bfloat16), "seq", 1).astype(carried.dtype)
            return (carried, grad_query + part_query)

        stacked, grad_query = lax.fori_loop(
            0, n_seq, return_step, (stacked, jnp.zeros((tok_dev, HEADS, head_dim), jnp.float32))
        )
        key_grad, value_grad = (stacked[2], stacked[3])
        grad_qkv_rows = jnp.concatenate(
            [grad_query.reshape(tok_dev, width), key_grad, value_grad], 1
        ).astype(jnp.bfloat16)
        sum_qkv = sum_qkv + jnp.einsum(
            "td,te->de", normed_one, grad_qkv_rows, preferred_element_type=jnp.float32
        )
        grad_normed_one = jnp.einsum(
            "te,de->td", grad_qkv_rows, back_qkv, preferred_element_type=jnp.float32
        )
        sum_gain_one = sum_gain_one + jnp.sum(grad_normed_one * scaled_one, 0)
        sum_bias_one = sum_bias_one + jnp.sum(grad_normed_one, 0)
        grad_input = grad_middle + norm_back(
            grad_normed_one, scaled_one, inv_one, back_gain_one.astype(jnp.float32)
        )
        input_grads.append(grad_input.astype(jnp.bfloat16))
    col_sums = (
        lax.psum_scatter(
            sum_qkv.astype(jnp.bfloat16), "seq", scatter_dimension=1, tiled=True
        ).astype(jnp.float32),
        lax.psum_scatter(
            sum_out.astype(jnp.bfloat16), "seq", scatter_dimension=1, tiled=True
        ).astype(jnp.float32),
        lax.psum_scatter(
            sum_up.astype(jnp.bfloat16), "seq", scatter_dimension=1, tiled=True
        ).astype(jnp.float32),
        lax.psum_scatter(
            sum_down.astype(jnp.bfloat16), "seq", scatter_dimension=1, tiled=True
        ).astype(jnp.float32),
    )
    reduced = (
        lax.psum_scatter(
            col_sums[0].astype(jnp.bfloat16), "dp", scatter_dimension=0, tiled=True
        ).astype(jnp.float32),
        lax.psum_scatter(
            col_sums[1].astype(jnp.bfloat16), "dp", scatter_dimension=0, tiled=True
        ).astype(jnp.float32),
        lax.psum_scatter(
            col_sums[2].astype(jnp.bfloat16), "dp", scatter_dimension=0, tiled=True
        ).astype(jnp.float32),
        lax.psum_scatter(
            col_sums[3].astype(jnp.bfloat16), "dp", scatter_dimension=0, tiled=True
        ).astype(jnp.float32),
        lax.psum_scatter(
            sum_gain_one.astype(jnp.bfloat16), "dp", scatter_dimension=0, tiled=True
        ).astype(jnp.float32),
        lax.psum_scatter(
            sum_bias_one.astype(jnp.bfloat16), "dp", scatter_dimension=0, tiled=True
        ).astype(jnp.float32),
        lax.psum_scatter(
            sum_gain_two.astype(jnp.bfloat16), "dp", scatter_dimension=0, tiled=True
        ).astype(jnp.float32),
        lax.psum_scatter(
            sum_bias_two.astype(jnp.bfloat16), "dp", scatter_dimension=0, tiled=True
        ).astype(jnp.float32),
    )
    norm_totals = lax.psum((reduced[4], reduced[5], reduced[6], reduced[7]), "seq")
    return (
        jnp.stack(out_rows),
        jnp.stack(input_grads),
        reduced[0],
        reduced[1],
        reduced[2],
        reduced[3],
        norm_totals[0],
        norm_totals[1],
        norm_totals[2],
        norm_totals[3],
    )


def solution(mesh):
    return jax.shard_map(
        shards,
        mesh=mesh,
        in_specs=(
            P(None, ("dp", "seq"), None),
            P(None, ("dp", "seq"), None),
            P("dp", "seq"),
            P("dp", "seq"),
            P("dp", "seq"),
            P("dp", "seq"),
            P("dp"),
            P("dp"),
            P("dp"),
            P("dp"),
            P(None, "dp", None),
            P(None, "dp", None),
        ),
        out_specs=(
            P(None, ("dp", "seq"), None),
            P(None, ("dp", "seq"), None),
            P("dp", "seq"),
            P("dp", "seq"),
            P("dp", "seq"),
            P("dp", "seq"),
            P("dp"),
            P("dp"),
            P("dp"),
            P("dp"),
        ),
        check_vma=False,
    )
```

```python
import jax
import jax.numpy as jnp
from jax import lax
from jax.sharding import PartitionSpec as P

HEADS = 17


EPS = 1e-05
GELU_C = 0.7978845608028654


def gelu_tanh(values):
    return 0.5 * values * (1.0 + jnp.tanh(GELU_C * (values + 0.044715 * values * values * values)))


def normalize(residual):
    row_mean = jnp.mean(residual, -1, keepdims=True)
    centered = residual - row_mean
    inv_std = lax.rsqrt(jnp.mean(centered * centered, -1, keepdims=True) + EPS)
    return (centered * inv_std, inv_std)


def norm_back(grad_normed, scaled, inv_std, gain_row):
    grad_scaled = grad_normed * gain_row
    return inv_std * (
        grad_scaled
        - jnp.mean(grad_scaled, -1, keepdims=True)
        - scaled * jnp.mean(grad_scaled * scaled, -1, keepdims=True)
    )


def running_total(counts):
    index = jnp.arange(counts.shape[0], dtype=jnp.int32)
    return jnp.sum(jnp.where(index[None, :] <= index[:, None], counts[None, :], 0), 1)


def segment_of(places, doc_ends):
    return jnp.sum((places[:, None] >= doc_ends[None, :]).astype(jnp.int32), 1)


def pair_swap(block):
    route = [(i, i ^ 1) for i in range(lax.axis_size("seq"))]
    return lax.ppermute(block, "seq", route)


def same_core():
    n_seq = lax.axis_size("seq")
    return [list(range(core, n_seq, 2)) for core in range(2)]


def gather_stack(shard):
    chips = lax.all_gather(shard, "seq", axis_index_groups=same_core())
    held = lax.all_gather(chips, "dp")
    other = pair_swap(held)
    first = lax.axis_index("seq") % 2 == 0
    both = jnp.stack([jnp.where(first, held, other), jnp.where(first, other, held)], 2)
    dp, chip_count = held.shape[:2]
    return both.transpose(1, 2, 0, 3, 4).reshape(2 * chip_count, dp, *shard.shape)


def pair_sum(parts):
    pairs = parts.reshape(parts.shape[0] // 2, 2, *parts.shape[1:])
    first = lax.axis_index("seq") % 2 == 0
    mine = jnp.where(first, pairs[:, 0], pairs[:, 1])
    other = jnp.where(first, pairs[:, 1], pairs[:, 0])
    got = pair_swap(other)
    return (mine.astype(jnp.float32) + got.astype(jnp.float32)).astype(jnp.bfloat16)


def scatter_stack(parts, after):
    held = pair_sum(parts).transpose(1, 0, 2, 3).reshape(-1, parts.shape[3])
    if after is not None:
        held, after = lax.optimization_barrier((held, after))
    held = lax.psum_scatter(held, "dp", scatter_dimension=0, tiled=True)
    held = lax.psum_scatter(
        held, "seq", scatter_dimension=0, axis_index_groups=same_core(), tiled=True
    )
    return held, after


def dot(left, right):
    return jnp.dot(left, right, preferred_element_type=jnp.float32)


def dot_right_t(left, right):
    return lax.dot_general(left, right, (((1,), (1,)), ((), ())), preferred_element_type=jnp.float32)


def dot_left_t(left, right):
    return lax.dot_general(left, right, (((0,), (0,)), ((), ())), preferred_element_type=jnp.float32)


def cols_of(rows, count):
    return rows.reshape(rows.shape[0], count, -1).transpose(1, 0, 2)


def apply_cols(rows, cols):
    lifted = jnp.broadcast_to(rows[None], (cols.shape[0],) + rows.shape)
    made = lax.dot_general(
        lifted, cols, (((2,), (1,)), ((0,), (0,))), preferred_element_type=jnp.float32
    )
    return made.transpose(1, 0, 2).reshape(rows.shape[0], -1)


def apply_cols_t(rows, cols):
    lifted = cols_of(rows, cols.shape[0])
    return lax.dot_general(
        lifted, cols, (((0, 2), (0, 2)), ((), ())), preferred_element_type=jnp.float32
    )


def grad_cols(left, right, count):
    lifted = jnp.broadcast_to(left[None], (count,) + left.shape)
    return lax.dot_general(
        lifted, cols_of(right, count), (((1,), (1,)), ((0,), (0,))),
        preferred_element_type=jnp.float32,
    )


def heads_of(rows, micro_count, head_dim):
    return rows.reshape(micro_count, -1, HEADS, head_dim).transpose(0, 2, 1, 3)


def rows_of(heads):
    micro_count, _, slots, head_dim = heads.shape
    return heads.transpose(0, 2, 1, 3).reshape(micro_count * slots, HEADS * head_dim)


def batched(left, right, left_dim, right_dim):
    return lax.dot_general(
        left,
        right,
        (((left_dim,), (right_dim,)), ((0, 1), (0, 1))),
        preferred_element_type=jnp.float32,
    )


def shards(
    tokens,
    cotangent,
    w_qkv,
    w_out,
    w_up,
    w_down,
    gain_one,
    bias_one,
    gain_two,
    bias_two,
    lengths,
    slot_order,
):
    micro_count, tok_dev, width = tokens.shape
    rows = micro_count * tok_dev
    head_dim = width // HEADS
    score_scale = head_dim ** (-0.5)
    n_seq = lax.axis_size("seq")
    my_slot = lax.axis_index("seq")
    bf16 = jnp.bfloat16

    norms = lax.all_gather(
        jnp.stack([gain_one, bias_one, gain_two, bias_two]), "dp", axis=1, tiled=True
    ).astype(jnp.float32)
    g_one, b_one, g_two, b_two = norms[0], norms[1], norms[2], norms[3]
    n_dp = lax.axis_size("dp")
    part, qkv_cols = w_qkv.shape
    out_cols = w_out.shape[1]
    up_cols = w_up.shape[1]
    fold = w_down.shape[0] // up_cols
    attn_stack = gather_stack(jnp.concatenate([w_qkv, w_out], 1))
    down_t = w_down.T
    ffn_stack = gather_stack(
        jnp.concatenate([w_up, *jnp.split(down_t, fold, 1)], 0)
    )
    cols_qkv = attn_stack[..., :qkv_cols].reshape(n_seq, width, qkv_cols)
    full_out = (
        attn_stack[..., qkv_cols:].reshape(n_seq, width, out_cols).transpose(1, 0, 2)
    ).reshape(width, width)
    cols_up = ffn_stack[:, :, :part].reshape(n_seq, width, up_cols)
    full_down_t = (
        ffn_stack[:, :, part:]
        .reshape(n_seq, n_dp, fold, out_cols, up_cols)
        .transpose(0, 3, 1, 2, 4)
        .reshape(width, fold * n_dp * up_cols)
    )

    doc_ends = jax.vmap(running_total)(lengths[:, 0])
    k_place = (
        slot_order[:, 0, :, None] * tok_dev + jnp.arange(tok_dev, dtype=jnp.int32)
    ).reshape(micro_count, n_seq * tok_dev)
    k_segment = jax.vmap(segment_of)(k_place, doc_ends)
    base_slot = lax.dynamic_slice_in_dim(slot_order[:, 0], my_slot, 1, 1)
    q_place = base_slot * tok_dev + jnp.arange(tok_dev, dtype=jnp.int32)
    q_segment = jax.vmap(segment_of)(q_place, doc_ends)
    allowed = (q_segment[:, :, None] == k_segment[:, None, :]) & (
        k_place[:, None, :] <= q_place[:, :, None]
    )

    residual = tokens.astype(jnp.float32).reshape(rows, width)
    scaled_one, inv_one = normalize(residual)
    normed_one = (scaled_one * g_one + b_one).astype(bf16)
    qkv_all = apply_cols(normed_one, cols_qkv).astype(bf16)
    queries = heads_of(qkv_all[:, :width], micro_count, head_dim)
    local_kv = qkv_all[:, width:].reshape(micro_count, tok_dev, 2 * width)
    group_kv = lax.all_gather(local_kv, "seq", axis=1, tiled=True)
    keys = heads_of(group_kv[..., :width], micro_count, head_dim)
    values = heads_of(group_kv[..., width:], micro_count, head_dim)

    scores = batched(queries, keys, 3, 3) * score_scale
    scores = jnp.where(allowed[:, None], scores, -jnp.inf)
    weights = jnp.exp(scores - jnp.max(scores, -1, keepdims=True))
    probs = weights * (1.0 / jnp.sum(weights, -1, keepdims=True))
    probs_low = probs.astype(bf16)
    attended = batched(probs_low, values, 3, 2)
    attn_flat = rows_of(attended.astype(bf16))
    middle = residual + dot(attn_flat, full_out)
    scaled_two, inv_two = normalize(middle)
    normed_two = (scaled_two * g_two + b_two).astype(bf16)
    hidden = apply_cols(normed_two, cols_up)
    activated_full, gelu_back = jax.vjp(gelu_tanh, hidden)
    activated = activated_full.astype(bf16)

    grad_rows = cotangent.reshape(rows, width)
    block_out = (middle + dot_right_t(activated, full_down_t)).astype(bf16)
    grad_hidden = gelu_back(dot(grad_rows, full_down_t))[0].astype(bf16)
    sum_down_t = dot_left_t(grad_rows, activated).astype(bf16)
    sum_down_t = (
        sum_down_t.reshape(n_seq, out_cols, n_dp, fold, up_cols)
        .transpose(0, 2, 3, 1, 4)
        .reshape(n_seq, n_dp, fold * out_cols, up_cols)
    )
    sum_up = grad_cols(normed_two, grad_hidden, n_seq).astype(bf16)
    sum_ffn, _ = scatter_stack(
        jnp.concatenate([sum_up.reshape(n_seq, n_dp, part, up_cols), sum_down_t], 2), None
    )
    grad_normed_two = apply_cols_t(grad_hidden, cols_up)
    grad_middle = grad_rows.astype(jnp.float32) + norm_back(
        grad_normed_two, scaled_two, inv_two, g_two
    )
    grad_branch = grad_middle.astype(bf16)
    sum_proj = grad_cols(attn_flat, grad_branch, n_seq).astype(bf16)
    grad_heads = heads_of(
        dot_right_t(grad_branch, full_out).astype(bf16), micro_count, head_dim
    )

    grad_probs = batched(grad_heads, values, 3, 3)
    row_dot = jnp.sum(probs * grad_probs, -1, keepdims=True)
    grad_scores = (probs * (grad_probs - row_dot)).astype(bf16)
    grad_query = rows_of(batched(grad_scores, keys, 3, 2) * score_scale)
    grad_keys = rows_of(batched(grad_scores, queries, 2, 2) * score_scale)
    grad_values = rows_of(batched(probs_low, grad_heads, 2, 2))
    grad_kv = jnp.concatenate([grad_keys.astype(bf16), grad_values.astype(bf16)], 1)
    grad_kv = grad_kv.reshape(micro_count, n_seq, tok_dev, 2 * width).transpose(1, 0, 2, 3)
    grad_kv = lax.psum_scatter(
        pair_sum(grad_kv), "seq", scatter_dimension=0, axis_index_groups=same_core()
    ).reshape(rows, 2 * width)
    grad_qkv_rows = jnp.concatenate([grad_query.astype(bf16), grad_kv], 1)
    sum_qkv = grad_cols(normed_one, grad_qkv_rows, n_seq).astype(bf16)
    sum_attn, sum_ffn = scatter_stack(
        jnp.concatenate([sum_qkv, sum_proj], 2).reshape(n_seq, n_dp, part, qkv_cols + out_cols),
        sum_ffn,
    )
    sum_attn = sum_attn.astype(jnp.float32)
    sum_ffn = sum_ffn.astype(jnp.float32)
    out_up = sum_ffn[:part]
    out_down = jnp.concatenate(jnp.split(sum_ffn[part:], fold, 0), 1).T
    out_qkv = sum_attn[:, :qkv_cols]
    out_proj = sum_attn[:, qkv_cols:]
    grad_normed_one = apply_cols_t(grad_qkv_rows, cols_qkv)
    grad_input = (
        grad_middle + norm_back(grad_normed_one, scaled_one, inv_one, g_one)
    ).astype(bf16)

    norm_sums = jnp.stack(
        [
            jnp.sum(grad_normed_one * scaled_one, 0),
            jnp.sum(grad_normed_one, 0),
            jnp.sum(grad_normed_two * scaled_two, 0),
            jnp.sum(grad_normed_two, 0),
        ]
    )
    norm_totals = lax.psum(norm_sums, ("dp", "seq"))
    norm_mine = lax.dynamic_slice_in_dim(norm_totals, lax.axis_index("dp") * part, part, 1)
    return (
        block_out.reshape(tokens.shape),
        grad_input.reshape(tokens.shape),
        out_qkv,
        out_proj,
        out_up,
        out_down,
        norm_mine[0],
        norm_mine[1],
        norm_mine[2],
        norm_mine[3],
    )


def solution(mesh):
    return jax.shard_map(
        shards,
        mesh=mesh,
        in_specs=(
            P(None, ("dp", "seq"), None),
            P(None, ("dp", "seq"), None),
            P("dp", "seq"),
            P("dp", "seq"),
            P("dp", "seq"),
            P("dp", "seq"),
            P("dp"),
            P("dp"),
            P("dp"),
            P("dp"),
            P(None, "dp", None),
            P(None, "dp", None),
        ),
        out_specs=(
            P(None, ("dp", "seq"), None),
            P(None, ("dp", "seq"), None),
            P("dp", "seq"),
            P("dp", "seq"),
            P("dp", "seq"),
            P("dp", "seq"),
            P("dp"),
            P("dp"),
            P("dp"),
            P("dp"),
        ),
        check_vma=False,
    )
```
